512 devices in a mesh: ia: 8 (over y), ja: 4 (over x), ka: 16 (over z, core).
Axes of the slice: x: 4, y: 8, z: 8, core: 2. Of those that a mesh axis runs over, the one named last changes fastest.
Arguments:
- tensor: bfloat16 [1024, 512, 2048], P('ia', 'ja', 'ka'), may hold values from -6144 to 6144
- factor_b: bfloat16 [64, 4, 128], P(None, 'ja', ('ia', 'ka')), may hold values from -60 to 60
- factor_c: bfloat16 [64, 16, 128], P(None, 'ka', ('ia', 'ja')), may hold values from -60 to 60
Outputs:
- final_a: float32 [64, 8, 128], P(None, 'ia', ('ja', 'ka'))
The draws below stay inside these ranges and needn't reach their ends.
All inputs are finite; a program needn't handle non-finite values.
Results may differ from the reference program's by a relative error of at most 0.00075.
Values may be sent and summed in bfloat16 or wider, within the bound.
A program may use at most 64 MiB of HBM per device.

```python
import math
import jax
import jax.numpy as jnp
from jax import lax

R = 64
I_DEV = 128
J_DEV = 128
K_DEV = 128
I = 1024
J = 512
K = 2048
N_IA = 8


def factor_rows(key, array_shape, row_count, growth, common):
    key_noise, key_shared, key_spread = jax.random.split(key, 3)
    random_part = jax.random.truncated_normal(key_noise, -4.0, 4.0, array_shape, jnp.float32)
    shared = jax.random.truncated_normal(key_shared, -4.0, 4.0, array_shape[1:], jnp.float32)
    spread = jax.random.uniform(key_spread, array_shape[1:], jnp.float32, 0.75, 1.25)
    position = jnp.arange(row_count, dtype=jnp.float32).reshape(array_shape[1:]) / row_count
    row_scale = jnp.exp(growth * position) * spread
    values = (random_part + common * shared[None]) * row_scale[None]
    return jnp.clip(values, -60.0, 60.0).astype(jnp.bfloat16)


def draw_factor_b(key, part):
    key = jax.random.fold_in(key, 11)
    return factor_rows(key, (R, J // J_DEV, J_DEV), J, math.log(3.0), 0.8)


def draw_factor_c(key, part):
    key = jax.random.fold_in(key, 23)
    return factor_rows(key, (R, K // K_DEV, K_DEV), K, math.log(3.0), 0.8)


def shard_levels(own_key, dims, cuts, low, largest):
    def one(dim, parts):
        draws = jax.random.uniform(jax.random.fold_in(jax.random.fold_in(own_key, 6), dim), (parts,), jnp.float32, low / len(cuts), largest / len(cuts))
        return jnp.repeat(jnp.exp(draws), dims[dim] // parts).reshape((-1,) + (1,) * (len(dims) - dim - 1))

    level = one(*cuts[0])
    for cut in cuts[1:]:
        level = level * one(*cut)
    return level


def normal_values(own_key, dims, scale, reach, cuts=(), kind=jnp.bfloat16):
    gain = shard_levels(own_key, dims, cuts, -0.22, 0.18) if cuts else 1.0
    result = jax.random.normal(own_key, dims, jnp.float32) * scale * gain
    return jnp.minimum(jnp.maximum(result, -reach), reach).astype(kind)


def setup_inputs(seed: int = 0) -> dict:
    key_of = jax.random.split(jax.random.key(seed), 4)
    tensor = normal_values(key_of[0], (I, J, K), (J * K // 1024), 6144.0, ((0, 8), (1, 4), (2, 16)))
    factor_b = draw_factor_b(jax.random.fold_in(key_of[3], 71), 0)
    factor_c = draw_factor_c(jax.random.fold_in(key_of[3], 71), 0)
    return {"tensor": tensor, "factor_b": factor_b, "factor_c": factor_c}


def gram_of(rows):
    return jnp.dot(rows.astype(jnp.float32), rows.T.astype(jnp.float32), preferred_element_type=jnp.float32)

def solve_with(matrix, right_side):
    lower = jnp.linalg.cholesky(matrix)
    return jax.scipy.linalg.cho_solve((lower, True), right_side)

def reference(tensor, factor_b, factor_c):
    rows_b = factor_b.reshape(R, J)
    rows_c = factor_c.reshape(R, K)
    blocks = tensor.reshape(N_IA, I_DEV, J, K)
    gram_b = gram_of(rows_b)
    gram_c = gram_of(rows_c)

    def mode_one(block):
        inner = lax.dot_general(rows_c.astype(jnp.float32), block.astype(jnp.float32), (((1,), (2,)), ((), ())), preferred_element_type=jnp.float32)
        return jnp.sum(inner * rows_b.astype(jnp.float32)[:, None, :], axis=2)
    pieces = lax.map(mode_one, blocks)
    new_a = solve_with(gram_b * gram_c, jnp.transpose(pieces, (1, 0, 2)).reshape(R, I))
    return new_a.reshape(R, N_IA, I_DEV)
```

```python
import functools

import jax
import jax.numpy as jnp
from jax import lax
from jax.experimental import pallas as pl
from jax.experimental.pallas import tpu as pltpu
from jax.sharding import PartitionSpec as P

MESH = pl.DeviceIdType.MESH
F32 = jnp.float32
BF16 = jnp.bfloat16
BLOCK = 8


def eliminate(state):
    rank = state.shape[0]
    row_of = lax.broadcasted_iota(jnp.int32, (rank, 128), 0)
    recips = jnp.zeros((rank, 128), F32)
    for first in range(0, rank, BLOCK):
        base = first // 8 * 8
        live = state[base:]
        rows = row_of[base:]
        columns = [jnp.broadcast_to(live[:, first + q : first + q + 1], live.shape) for q in range(BLOCK)]
        marks = recips[base:]
        for q in range(BLOCK):
            at = first + q - base
            recip = 1.0 / columns[q][at : at + 1]
            marks = jnp.where(rows == first + q, recip, marks)
            lower = jnp.where(rows > first + q, columns[q] * recip, 0.0)
            for later in range(q + 1, BLOCK):
                columns[later] = columns[later] - lower * columns[later][at : at + 1]
            live = live - lower * live[at : at + 1]
        state = live if base == 0 else jnp.concatenate([state[:base], live], axis=0)
        recips = marks if base == 0 else jnp.concatenate([recips[:base], marks], axis=0)
    return state, recips


def kernel(
    sizes, tensor_ref, b_ref, c_ref, out_ref,
    tensor, piece, seen, tile_b, tile_c, slab_b, slab_c, gram_b, gram_c, partial, partials,
    load_sem, send_sem, recv_sem,
):
    n_ia, n_ja, n_ka = sizes
    ia, ja, ka = (lax.axis_index(a) for a in ("ia", "ja", "ka"))
    n_own = n_ja * n_ka

    load = pltpu.make_async_copy(tensor_ref, tensor, load_sem)
    load.start()

    def along_y(d):
        return {"ia": lax.rem(ia + d, n_ia)}

    def along_x(d):
        return {"ja": lax.rem(ja + d, n_ja)}

    def along_z(d):
        return {"ka": lax.rem(ka + d, n_ka)}

    barrier = pltpu.get_barrier_semaphore()
    for count, place in ((n_ia, along_y), (n_ja, along_x), (n_ka, along_z)):
        for d in range(1, count):
            pl.semaphore_signal(barrier, inc=1, device_id=place(d), device_id_type=MESH)

    lane = lax.broadcasted_iota(jnp.int32, (128, 128), 1)
    own_c = c_ref[0].astype(F32)
    own_b = b_ref[0].astype(F32)
    piece[0:4, :] = jnp.concatenate([own_c, own_c], axis=1)
    piece[4:5, :] = jnp.concatenate([own_b, own_b], axis=1)
    seen[pl.ds(pl.multiple_of(ia * 8, 8), 8), :] = piece[...]

    pl.semaphore_wait(barrier, n_ia + n_ja + n_ka - 3)

    def send(source, target, stage, place):
        copy = pltpu.make_async_remote_copy(
            src_ref=source, dst_ref=target, send_sem=send_sem.at[stage], recv_sem=recv_sem.at[stage],
            device_id=place, device_id_type=MESH,
        )
        copy.start()

    def wait(buffer, rows, sem):
        part = buffer.at[pl.ds(0, rows)]
        pltpu.make_async_copy(part, part, sem).wait()

    for d in range(1, n_ia):
        send(piece, seen.at[pl.ds(pl.multiple_of(ia * 8, 8), 8)], 0, along_y(d))
    wait(seen, 8 * (n_ia - 1), recv_sem.at[0])

    at_b = pl.ds(pl.multiple_of(ka * 8, 8), 8)
    at_c = pl.ds(pl.multiple_of(ja * 32, 32), 32)
    for q in range(4):
        tile_c[8 * q : 8 * q + 8, :] = seen[pl.ds(q, 8, stride=8), :]
    tile_b[...] = seen[pl.ds(4, 8, stride=8), :]
    for d in range(1, n_ja):
        send(tile_c, slab_c.at[at_c], 1, along_x(d))
    for d in range(1, n_ka):
        send(tile_b, slab_b.at[at_b], 2, along_z(d))
    slab_c[at_c, :] = tile_c[...]
    slab_b[at_b, :] = tile_b[...]
    wait(slab_c, 32 * (n_ja - 1), recv_sem.at[1])

    def packed_gram(slab):
        rows = slab.astype(BF16)
        full = lax.dot_general(rows, rows, (((0,), (0,)), ((), ())), preferred_element_type=F32)
        return jnp.where(lane[:32] < 64, full[0:32], full[32:64])

    at_gram_c = pl.ds(pl.multiple_of(ka * 32, 32), 32)
    at_gram_b = pl.ds(pl.multiple_of(ja * 32, 32), 32)
    gram_c[at_gram_c, :] = packed_gram(slab_c[...])
    for d in range(1, n_ka):
        send(gram_c.at[at_gram_c], gram_c.at[at_gram_c], 3, along_z(d))
    wait(slab_b, 8 * (n_ka - 1), recv_sem.at[2])
    gram_b[at_gram_b, :] = packed_gram(slab_b[...])
    for d in range(1, n_ja):
        send(gram_b.at[at_gram_b], gram_b.at[at_gram_b], 4, along_x(d))

    order_b = jnp.concatenate([slab_b[pl.ds(i, 16, stride=8), :] for i in range(8)], axis=0)
    order_c = jnp.concatenate([slab_c[pl.ds(i, 16, stride=8), :] for i in range(8)], axis=0)
    weights = jnp.concatenate(
        [jnp.where(lane < 64, order_c, 0.0), jnp.where(lane >= 64, order_c, 0.0)], axis=0
    ).astype(BF16)
    load.wait()

    def contract(p, _):
        both = jnp.concatenate([tensor[2 * p], tensor[2 * p + 1]], axis=1)
        inner = jnp.dot(both, weights, preferred_element_type=F32)
        row = jnp.sum(inner * order_b, axis=0, keepdims=True)
        partial[p, 0:1, :] = row
        return 0

    lax.fori_loop(0, n_own, contract, 0, unroll=4)

    me = ja * n_ka + ka

    def hand(d, _):
        owner = lax.rem(me + d, n_own)
        send(
            partial.at[owner, pl.ds(0, 1)], partials.at[me, pl.ds(0, 1)], 5,
            {"ja": lax.div(owner, n_ka), "ka": lax.rem(owner, n_ka)},
        )
        return 0

    lax.fori_loop(1, n_own, hand, 0)
    partials[me, 0:1, :] = partial[me, 0:1, :]

    wait(gram_c, 32 * (n_ka - 1), recv_sem.at[3])
    total_c = gram_c[0:32, :]
    for k in range(1, n_ka):
        total_c = total_c + gram_c[32 * k : 32 * k + 32, :]
    wait(gram_b, 32 * (n_ja - 1), recv_sem.at[4])
    total_b = gram_b[0:32, :]
    for j in range(1, n_ja):
        total_b = total_b + gram_b[32 * j : 32 * j + 32, :]
    matrix = total_b * total_c
    square = jnp.concatenate([matrix, pltpu.roll(matrix, 64, 1)], axis=0)
    row64 = lax.broadcasted_iota(jnp.int32, (64, 128), 0)
    lane64 = lane[:64]
    state = jnp.where(lane64 < 64, square, jnp.where(lane64 - 64 == row64, 1.0, 0.0))
    state, recips = eliminate(state)
    inverse = jnp.where(lane64 < 64, pltpu.roll(state, 64, 1), state)

    part = partials.at[pl.ds(0, n_own - 1), pl.ds(0, 1)]
    pltpu.make_async_copy(part, part, recv_sem.at[5]).wait()
    right = jnp.sum(partials[:, 0, :], axis=0, keepdims=True)
    products = inverse * right
    first = jnp.sum(jnp.where(lane64 < 64, products, 0.0), axis=1, keepdims=True)
    second = jnp.sum(jnp.where(lane64 < 64, 0.0, products), axis=1, keepdims=True)
    middle = jnp.where(lane64 < 64, first, second) * recips
    answer = jnp.sum(inverse * middle, axis=0, keepdims=True)
    out_ref[0, 0:1, :] = answer[:, :64]
    out_ref[0, 1:2, :] = answer[:, 64:]

    wait(seen, 8 * (n_ia - 1), send_sem.at[0])
    wait(slab_c, 32 * (n_ja - 1), send_sem.at[1])
    wait(slab_b, 8 * (n_ka - 1), send_sem.at[2])
    wait(gram_c, 32 * (n_ka - 1), send_sem.at[3])
    wait(gram_b, 32 * (n_ja - 1), send_sem.at[4])
    pltpu.make_async_copy(part, part, send_sem.at[5]).wait()


def shards(sizes, tensor, factor_b, factor_c):
    n_ia, n_ja, n_ka = sizes
    vmem = pl.BlockSpec(memory_space=pltpu.VMEM)
    out = pl.pallas_call(
        functools.partial(kernel, sizes),
        name="als_update",
        out_shape=jax.ShapeDtypeStruct((1, 2, 64), F32),
        in_specs=[pl.BlockSpec(memory_space=pl.ANY), vmem, vmem],
        out_specs=vmem,
        scratch_shapes=[
            pltpu.VMEM((128, 128, 128), BF16),
            pltpu.VMEM((8, 128), F32),
            pltpu.VMEM((8 * n_ia, 128), F32),
            pltpu.VMEM((8, 128), F32),
            pltpu.VMEM((32, 128), F32),
            pltpu.VMEM((8 * n_ka, 128), F32),
            pltpu.VMEM((32 * n_ja, 128), F32),
            pltpu.VMEM((32 * n_ja, 128), F32),
            pltpu.VMEM((32 * n_ka, 128), F32),
            pltpu.VMEM((n_ja * n_ka, 8, 128), F32),
            pltpu.VMEM((n_ja * n_ka, 8, 128), F32),
            pltpu.SemaphoreType.DMA,
            pltpu.SemaphoreType.DMA((6,)),
            pltpu.SemaphoreType.DMA((6,)),
        ],
        compiler_params=pltpu.CompilerParams(
            collective_id=0, has_side_effects=True, vmem_limit_bytes=48 * 1024 * 1024
        ),
    )(tensor, jnp.transpose(factor_b, (1, 2, 0)), jnp.transpose(factor_c, (1, 2, 0)))
    return jnp.transpose(out, (2, 0, 1))


def solution(mesh):
    sizes = tuple(mesh.shape[a] for a in ("ia", "ja", "ka"))
    in_specs = (P("ia", "ja", "ka"), P(None, "ja", ("ia", "ka")), P(None, "ka", ("ia", "ja")))
    out_specs = P(None, "ia", ("ja", "ka"))
    return jax.shard_map(
        functools.partial(shards, sizes), mesh=mesh, in_specs=in_specs, out_specs=out_specs, check_vma=False
    )
```

```python
import functools

import jax
import jax.numpy as jnp
from jax import lax
from jax.experimental import pallas as pl
from jax.experimental.pallas import tpu as pltpu
from jax.sharding import PartitionSpec as P

MESH = pl.DeviceIdType.MESH
F32 = jnp.float32
BF16 = jnp.bfloat16
BLOCK = 8


def eliminate(state):
    rank = state.shape[0]
    row_of = lax.broadcasted_iota(jnp.int32, (rank, 128), 0)
    recips = jnp.zeros((rank, 128), F32)
    for first in range(0, rank, BLOCK):
        base = first // 8 * 8
        live = state[base:]
        rows = row_of[base:]
        columns = [jnp.broadcast_to(live[:, first + q : first + q + 1], live.shape) for q in range(BLOCK)]
        marks = recips[base:]
        for q in range(BLOCK):
            at = first + q - base
            recip = 1.0 / columns[q][at : at + 1]
            marks = jnp.where(rows == first + q, recip, marks)
            lower = jnp.where(rows > first + q, columns[q] * recip, 0.0)
            for later in range(q + 1, BLOCK):
                columns[later] = columns[later] - lower * columns[later][at : at + 1]
            live = live - lower * live[at : at + 1]
        state = live if base == 0 else jnp.concatenate([state[:base], live], axis=0)
        recips = marks if base == 0 else jnp.concatenate([recips[:base], marks], axis=0)
    return state, recips


def far_first(count):
    return sorted(range(1, count), key=lambda d: -min(d, count - d))


def kernel(
    sizes, tensor_ref, b_ref, c_ref, out_ref,
    tensor, own_b, own_c, piece, seen, tile_b, tile_c, slab_b, slab_c, wide_c, gram_b, gram_c, matrix, partial, partials,
    load_sem, ready, send_sem, recv_sem,
):
    n_ia, n_ja, n_ka = sizes
    n_z = n_ka // 2
    ia, ja, ka = (lax.axis_index(a) for a in ("ia", "ja", "ka"))
    z, core = lax.div(ka, 2), lax.rem(ka, 2)
    n_own = n_ja * n_ka

    load_c = pltpu.make_async_copy(c_ref, own_c, load_sem.at[0])
    load_b = pltpu.make_async_copy(b_ref, own_b, load_sem.at[1])
    load = pltpu.make_async_copy(tensor_ref, tensor, load_sem.at[2])
    load_c.start()
    load_b.start()

    def along_y(d):
        return {"ia": lax.rem(ia + d, n_ia)}

    def along_x(dx, dc):
        return {"ja": lax.rem(ja + dx, n_ja), "ka": 2 * z + lax.rem(core + dc, 2)}

    def along_z(d):
        return {"ka": 2 * lax.rem(z + d, n_z) + core}

    ys = far_first(n_ia)
    zs = far_first(n_z)
    xs = [(dx, dc) for dx in far_first(n_ja) + [0] for dc in (0, 1) if dx or dc]

    barrier = pltpu.get_barrier_semaphore()

    def signal(sem, place):
        pl.semaphore_signal(sem, inc=1, device_id=place, device_id_type=MESH)

    for d in ys:
        signal(barrier, along_y(d))
    for dx, dc in xs:
        signal(barrier, along_x(dx, dc))

    def greet_higher(k, _):
        signal(barrier, {"ka": k})
        return 0

    lax.fori_loop(2 * z + 2, n_ka, greet_higher, 0)
    load.start()

    load_c.wait()
    load_b.wait()
    lane = lax.broadcasted_iota(jnp.int32, (128, 128), 1)
    c_rows = own_c[0].astype(F32)
    b_row = own_b[0].astype(F32)
    piece[0:4, :] = jnp.concatenate([c_rows, c_rows], axis=1)
    piece[4:5, :] = jnp.concatenate([b_row, b_row], axis=1)
    seen[pl.ds(pl.multiple_of(ia * 8, 8), 8), :] = piece[...]

    pl.semaphore_wait(barrier, n_ia - 1 + 2 * n_ja - 1 + 2 * z)

    def greet_lower(k, _):
        signal(ready, {"ka": k})
        return 0

    sent = []

    def send(source, target, stage, place):
        pltpu.make_async_remote_copy(
            src_ref=source, dst_ref=target, send_sem=send_sem.at[stage], recv_sem=recv_sem.at[stage],
            device_id=place, device_id_type=MESH,
        ).start()

    def wait(part, sem):
        pltpu.make_async_copy(part, part, sem).wait()

    for d in ys:
        send(piece, seen.at[pl.ds(pl.multiple_of(ia * 8, 8), 8)], 0, along_y(d))
    lax.fori_loop(0, 2 * z, greet_lower, 0)
    part = seen.at[pl.ds(0, 8 * (n_ia - 1))]
    sent.append((part, 0))
    wait(part, recv_sem.at[0])

    at_b = pl.ds(pl.multiple_of(ka * 8, 8), 8)
    at_c = pl.ds(pl.multiple_of((core * n_ja + ja) * 32, 32), 32)
    tile_c[...] = jnp.concatenate([seen[pl.ds(q, 8, stride=8), :] for q in range(4)], axis=0).astype(BF16)
    tile_b[...] = seen[pl.ds(4, 8, stride=8), :]
    for dx, dc in xs:
        send(tile_c, slab_c.at[at_c], 1, along_x(dx, dc))

    def send_b(k, _):
        send(tile_b, slab_b.at[at_b], 2, {"ka": k})
        return 0

    lax.fori_loop(0, 2 * z, send_b, 0)
    send_b(2 * z + 1 - core, 0)

    @pl.when(z < n_z - 1)
    def _():
        pl.semaphore_wait(ready, n_ka - 2 - 2 * z)

    lax.fori_loop(2 * z + 2, n_ka, send_b, 0)
    slab_c[at_c, :] = tile_c[...]
    slab_b[at_b, :] = tile_b[...]
    part = slab_c.at[pl.ds(0, 32 * (2 * n_ja - 1))]
    sent.append((part, 1))
    wait(part, recv_sem.at[1])

    def packed_gram(rows):
        full = lax.dot_general(rows, rows, (((0,), (0,)), ((), ())), preferred_element_type=F32)
        both = jnp.where(lane[:32] < 64, full[0:32], full[32:64])
        return jnp.where(core == 0, both[0:16], both[16:32])

    at_gram_c = pl.ds(pl.multiple_of(z * 16, 16), 16)
    at_gram_b = pl.ds(pl.multiple_of(ja * 16, 16), 16)
    gram_c[at_gram_c, :] = packed_gram(slab_c[...])
    for d in zs:
        send(gram_c.at[at_gram_c], gram_c.at[at_gram_c], 3, along_z(d))
    part_c = gram_c.at[pl.ds(0, 16 * (n_z - 1))]
    wide_c[...] = slab_c[pl.ds(pl.multiple_of(core * n_ja * 32, 32), n_ja * 32), :].astype(F32)
    order_c = jnp.concatenate([wide_c[pl.ds(i, 16, stride=8), :] for i in range(8)], axis=0)
    weights = jnp.concatenate(
        [jnp.where(lane < 64, order_c, 0.0), jnp.where(lane >= 64, order_c, 0.0)], axis=0
    ).astype(BF16)
    load.wait()
    part = slab_b.at[pl.ds(0, 8 * (n_ka - 1))]
    sent.append((part, 2))
    wait(part, recv_sem.at[2])
    order_b = jnp.concatenate([slab_b[pl.ds(i, 16, stride=8), :] for i in range(8)], axis=0)

    me = ja * n_ka + ka

    def contract(step, _):
        dz = n_z // 2 + lax.div(step + 1, 2) * (1 - 2 * lax.rem(step, 2))
        owners = [
            (dx, dc, lax.rem(ja + dx, n_ja), 2 * lax.rem(z + dz, n_z) + lax.rem(core + dc, 2))
            for dx in far_first(n_ja) + [0]
            for dc in (1, 0)
        ]
        for dx, dc, x, k in owners:
            p = x * n_ka + k
            both = jnp.concatenate([tensor[2 * p], tensor[2 * p + 1]], axis=1)
            inner = jnp.dot(both, weights, preferred_element_type=F32)
            partial[p, 0:1, :] = jnp.sum(inner * order_b, axis=0, keepdims=True)
        for dx, dc, x, k in owners:
            p = x * n_ka + k

            def hand(x=x, k=k, p=p):
                send(partial.at[p, pl.ds(0, 1)], partials.at[me, pl.ds(0, 1)], 5, {"ja": x, "ka": k})

            if dx or dc:
                hand()
            else:
                pl.when(step < n_z - 1)(hand)
        return 0

    lax.fori_loop(0, n_z, contract, 0)
    partials[me, 0:1, :] = partial[me, 0:1, :]
    part_r = partials.at[pl.ds(0, n_own - 1), pl.ds(0, 1)]

    gram_b[at_gram_b, :] = packed_gram(slab_b[...].astype(BF16))
    for d in far_first(n_ja):
        send(gram_b.at[at_gram_b], gram_b.at[at_gram_b], 4, along_x(d, 0))
    part_b = gram_b.at[pl.ds(0, 16 * (n_ja - 1))]
    sent += [(part_c, 3), (part_b, 4), (part_r, 5)]

    wait(part_c, recv_sem.at[3])
    total_c = gram_c[0:16, :]
    for k in range(1, n_z):
        total_c = total_c + gram_c[16 * k : 16 * k + 16, :]
    wait(part_b, recv_sem.at[4])
    total_b = gram_b[0:16, :]
    for j in range(1, n_ja):
        total_b = total_b + gram_b[16 * j : 16 * j + 16, :]
    at_half = pl.ds(pl.multiple_of(core * 16, 16), 16)
    matrix[at_half, :] = total_b * total_c
    send(matrix.at[at_half], matrix.at[at_half], 6, along_x(0, 1))
    part = matrix.at[pl.ds(0, 16)]
    sent.append((part, 6))
    wait(part, recv_sem.at[6])
    packed = matrix[...]
    square = jnp.concatenate([packed, pltpu.roll(packed, 64, 1)], axis=0)
    row64 = lax.broadcasted_iota(jnp.int32, (64, 128), 0)
    lane64 = lane[:64]
    state = jnp.where(lane64 < 64, square, jnp.where(lane64 - 64 == row64, 1.0, 0.0))
    state, recips = eliminate(state)
    inverse = jnp.where(lane64 < 64, pltpu.roll(state, 64, 1), state)

    wait(part_r, recv_sem.at[5])
    right = jnp.sum(partials[:, 0, :], axis=0, keepdims=True)
    products = inverse * right
    first = jnp.sum(jnp.where(lane64 < 64, products, 0.0), axis=1, keepdims=True)
    second = jnp.sum(jnp.where(lane64 < 64, 0.0, products), axis=1, keepdims=True)
    middle = jnp.where(lane64 < 64, first, second) * recips
    answer = jnp.sum(inverse * middle, axis=0, keepdims=True)
    out_ref[0, 0:1, :] = answer[:, :64]
    out_ref[0, 1:2, :] = answer[:, 64:]

    for part, stage in sent:
        wait(part, send_sem.at[stage])


def shards(sizes, tensor, factor_b, factor_c):
    n_ia, n_ja, n_ka = sizes
    arrays = (tensor, jnp.transpose(factor_b, (1, 2, 0)), jnp.transpose(factor_c, (1, 2, 0)))
    in_hbm = pl.BlockSpec(memory_space=pltpu.HBM)
    out = pl.pallas_call(
        functools.partial(kernel, sizes),
        name="als_update",
        out_shape=jax.ShapeDtypeStruct((1, 2, 64), F32),
        in_specs=[in_hbm, in_hbm, in_hbm],
        out_specs=pl.BlockSpec(memory_space=pltpu.VMEM),
        scratch_shapes=[
            pltpu.VMEM((128, 128, 128), BF16),
            pltpu.VMEM((1, 1, 64), BF16),
            pltpu.VMEM((1, 4, 64), BF16),
            pltpu.VMEM((8, 128), F32),
            pltpu.VMEM((8 * n_ia, 128), F32),
            pltpu.VMEM((8, 128), F32),
            pltpu.VMEM((32, 128), BF16),
            pltpu.VMEM((8 * n_ka, 128), F32),
            pltpu.VMEM((2 * 32 * n_ja, 128), BF16),
            pltpu.VMEM((32 * n_ja, 128), F32),
            pltpu.VMEM((16 * n_ja, 128), F32),
            pltpu.VMEM((16 * n_ka // 2, 128), F32),
            pltpu.VMEM((32, 128), F32),
            pltpu.VMEM((n_ja * n_ka, 8, 128), F32),
            pltpu.VMEM((n_ja * n_ka, 8, 128), F32),
            pltpu.SemaphoreType.DMA((3,)),
            pltpu.SemaphoreType.REGULAR,
            pltpu.SemaphoreType.DMA((7,)),
            pltpu.SemaphoreType.DMA((7,)),
        ],
        compiler_params=pltpu.CompilerParams(
            collective_id=0, has_side_effects=True, vmem_limit_bytes=48 * 1024 * 1024
        ),
    )(*(pltpu.with_memory_space_constraint(array, pltpu.HBM) for array in arrays))
    return jnp.transpose(out, (2, 0, 1))


def solution(mesh):
    sizes = tuple(mesh.shape[a] for a in ("ia", "ja", "ka"))
    in_specs = (P("ia", "ja", "ka"), P(None, "ja", ("ia", "ka")), P(None, "ka", ("ia", "ja")))
    out_specs = P(None, "ia", ("ja", "ka"))
    return jax.shard_map(
        functools.partial(shards, sizes), mesh=mesh, in_specs=in_specs, out_specs=out_specs, check_vma=False
    )
```

```python
import functools

import jax
import jax.numpy as jnp
from jax import lax
from jax.experimental import pallas as pl
from jax.experimental.pallas import tpu as pltpu
from jax.sharding import PartitionSpec as P

MESH = pl.DeviceIdType.MESH
F32 = jnp.float32
BF16 = jnp.bfloat16
BLOCK = 16


def eliminate(state):
    rank = state.shape[0]
    row_of = lax.broadcasted_iota(jnp.int32, (rank, 128), 0)
    recips = jnp.zeros((rank, 128), F32)
    for first in range(0, rank, BLOCK):
        base = first // 8 * 8
        live = state[base:]
        rows = row_of[base:]
        columns = [jnp.broadcast_to(live[:, first + q : first + q + 1], live.shape) for q in range(BLOCK)]
        marks = recips[base:]
        for q in range(BLOCK):
            at = first + q - base
            recip = 1.0 / columns[q][at : at + 1]
            marks = jnp.where(rows == first + q, recip, marks)
            lower = jnp.where(rows > first + q, columns[q] * recip, 0.0)
            for later in range(q + 1, BLOCK):
                columns[later] = columns[later] - lower * columns[later][at : at + 1]
            live = live - lower * live[at : at + 1]
        state = live if base == 0 else jnp.concatenate([state[:base], live], axis=0)
        recips = marks if base == 0 else jnp.concatenate([recips[:base], marks], axis=0)
    return state, recips


def far_first(count):
    return sorted(range(1, count), key=lambda d: -min(d, count - d))


def kernel(
    sizes, tensor_ref, b_ref, c_ref, out_ref,
    tensor, own_b, own_c, piece, seen, tile_b, tile_c, slab_b, slab_c, wide_c, gram_b, gram_c, matrix, inner, partial, partials,
    load_sem, ready, send_sem, recv_sem,
):
    n_ia, n_ja, n_ka = sizes
    n_z = n_ka // 2
    ia, ja, ka = (lax.axis_index(a) for a in ("ia", "ja", "ka"))
    z, core = lax.div(ka, 2), lax.rem(ka, 2)
    n_own = n_ja * n_ka
    half = n_z // 2

    load_c = pltpu.make_async_copy(c_ref, own_c, load_sem.at[0])
    load_b = pltpu.make_async_copy(b_ref, own_b, load_sem.at[1])
    load = pltpu.make_async_copy(tensor_ref, tensor, load_sem.at[2])
    load_c.start()
    load_b.start()

    def along_y(d):
        return {"ia": lax.rem(ia + d, n_ia)}

    def along_x(dx, dc):
        return {"ja": lax.rem(ja + dx, n_ja), "ka": 2 * z + lax.rem(core + dc, 2)}

    ys = far_first(n_ia)
    xs = [(dx, dc) for dx in far_first(n_ja) + [0] for dc in (0, 1) if dx or dc]

    barrier = pltpu.get_barrier_semaphore()

    def signal(sem, place):
        pl.semaphore_signal(sem, inc=1, device_id=place, device_id_type=MESH)

    for d in ys:
        signal(barrier, along_y(d))
    signal(barrier, along_x(0, 1))

    def greet_higher_x(x, _):
        for c in (0, 1):
            signal(barrier, {"ja": x, "ka": 2 * z + c})
        return 0

    lax.fori_loop(ja + 1, n_ja, greet_higher_x, 0)

    def greet_higher(k, _):
        signal(barrier, {"ka": k})
        return 0

    lax.fori_loop(2 * z + 2, n_ka, greet_higher, 0)
    load.start()

    load_c.wait()
    load_b.wait()
    lane = lax.broadcasted_iota(jnp.int32, (128, 128), 1)
    c_rows = own_c[0].astype(F32)
    b_row = own_b[0].astype(F32)
    piece[0:4, :] = jnp.concatenate([c_rows, c_rows], axis=1)
    piece[4:5, :] = jnp.concatenate([b_row, b_row], axis=1)
    seen[pl.ds(pl.multiple_of(ia * 8, 8), 8), :] = piece[...]

    pl.semaphore_wait(barrier, n_ia + 2 * ja + 2 * z)

    def greet_lower(k, _):
        signal(ready.at[0], {"ka": k})
        return 0

    def greet_lower_x(x, _):
        for c in (0, 1):
            signal(ready.at[1], {"ja": x, "ka": 2 * z + c})
        return 0

    sent = []

    def send(source, target, stage, place):
        pltpu.make_async_remote_copy(
            src_ref=source, dst_ref=target, send_sem=send_sem.at[stage], recv_sem=recv_sem.at[stage],
            device_id=place, device_id_type=MESH,
        ).start()

    def wait(part, sem):
        pltpu.make_async_copy(part, part, sem).wait()

    for d in ys:
        send(piece, seen.at[pl.ds(pl.multiple_of(ia * 8, 8), 8)], 0, along_y(d))
    lax.fori_loop(0, 2 * z, greet_lower, 0)
    lax.fori_loop(0, ja, greet_lower_x, 0)
    part = seen.at[pl.ds(0, 8 * (n_ia - 1))]
    sent.append((part, 0))
    wait(part, recv_sem.at[0])

    @pl.when(ja < n_ja - 1)
    def _():
        pl.semaphore_wait(ready.at[1], 2 * (n_ja - 1 - ja))


    at_b = pl.ds(pl.multiple_of(ka * 8, 8), 8)
    at_c = pl.ds(pl.multiple_of((core * n_ja + ja) * 32, 32), 32)
    tile_c[...] = jnp.concatenate([seen[pl.ds(q, 8, stride=8), :] for q in range(4)], axis=0).astype(BF16)
    tile_b[...] = seen[pl.ds(4, 8, stride=8), :]
    for dx, dc in xs:
        send(tile_c, slab_c.at[at_c], 1, along_x(dx, dc))

    def send_b(k, _):
        send(tile_b, slab_b.at[at_b], 2, {"ka": k})
        return 0

    lax.fori_loop(0, 2 * z, send_b, 0)
    send_b(2 * z + 1 - core, 0)

    @pl.when(z < n_z - 1)
    def _():
        pl.semaphore_wait(ready.at[0], n_ka - 2 - 2 * z)

    lax.fori_loop(2 * z + 2, n_ka, send_b, 0)
    slab_c[at_c, :] = tile_c[...]
    slab_b[at_b, :] = tile_b[...]
    part = slab_c.at[pl.ds(0, 32 * (2 * n_ja - 1))]
    sent.append((part, 1))
    wait(part, recv_sem.at[1])

    def packed_gram(rows):
        full = lax.dot_general(rows, rows, (((0,), (0,)), ((), ())), preferred_element_type=F32)
        both = jnp.where(lane[:32] < 64, full[0:32], full[32:64])
        return jnp.where(core == 0, both[0:16], both[16:32])

    at_gram_c = pl.ds(pl.multiple_of(z * 16, 16), 16)
    at_gram_b = pl.ds(pl.multiple_of(ja * 16, 16), 16)
    gram_c[at_gram_c, :] = packed_gram(slab_c[...])

    def send_gram(to_z, _):
        @pl.when(to_z != z)
        def _():
            send(gram_c.at[at_gram_c], gram_c.at[at_gram_c], 3, {"ka": 2 * to_z + core})

        return 0

    lax.fori_loop(0, n_z, send_gram, 0)
    part_c = gram_c.at[pl.ds(0, 16 * (n_z - 1))]
    wide_c[...] = slab_c[pl.ds(pl.multiple_of(core * n_ja * 32, 32), n_ja * 32), :].astype(F32)
    order_c = jnp.concatenate([wide_c[pl.ds(i, 16, stride=8), :] for i in range(8)], axis=0)
    weights = jnp.concatenate(
        [jnp.where(lane < 64, order_c, 0.0), jnp.where(lane >= 64, order_c, 0.0)], axis=0
    ).astype(BF16)
    load.wait()

    def product(p):
        both = jnp.concatenate([tensor[2 * p], tensor[2 * p + 1]], axis=1)
        return jnp.dot(both, weights, preferred_element_type=F32)

    def contract(p, _):
        inner[p] = product(p)
        return 0

    @pl.when(z < half)
    def _():
        lax.fori_loop(0, n_own, contract, 0, unroll=4)

    part = slab_b.at[pl.ds(0, 8 * (n_ka - 1))]
    sent.append((part, 2))
    wait(part, recv_sem.at[2])

    gram_b[at_gram_b, :] = packed_gram(slab_b[...].astype(BF16))
    for d in far_first(n_ja):
        send(gram_b.at[at_gram_b], gram_b.at[at_gram_b], 4, along_x(d, 0))
    part_b = gram_b.at[pl.ds(0, 16 * (n_ja - 1))]

    order_b = jnp.concatenate([slab_b[pl.ds(i, 16, stride=8), :] for i in range(8)], axis=0)
    me = ja * n_ka + ka

    def weigh(made, to_z, _):
        owners = [
            (dx, dc, lax.rem(ja + dx, n_ja), 2 * to_z + lax.rem(core + dc, 2))
            for dx in far_first(n_ja) + [0]
            for dc in (1, 0)
        ]
        for dx, dc, x, k in owners:
            p = x * n_ka + k
            partial[p, 0:1, :] = jnp.sum(made(p) * order_b, axis=0, keepdims=True)
        for dx, dc, x, k in owners:
            p = x * n_ka + k

            def hand(x=x, k=k, p=p):
                send(partial.at[p, pl.ds(0, 1)], partials.at[me, pl.ds(0, 1)], 5, {"ja": x, "ka": k})

            if dx or dc:
                hand()
            else:
                pl.when(to_z != z)(hand)
        return 0

    @pl.when(z < half)
    def _():
        lax.fori_loop(0, n_z, functools.partial(weigh, lambda p: inner[p]), 0)

    @pl.when(z >= half)
    def _():
        lax.fori_loop(0, n_z, functools.partial(weigh, product), 0)

    partials[me, 0:1, :] = partial[me, 0:1, :]
    part_r = partials.at[pl.ds(0, n_own - 1), pl.ds(0, 1)]
    sent += [(part_c, 3), (part_b, 4), (part_r, 5)]

    wait(part_c, recv_sem.at[3])
    total_c = gram_c[0:16, :]
    for k in range(1, n_z):
        total_c = total_c + gram_c[16 * k : 16 * k + 16, :]
    wait(part_b, recv_sem.at[4])
    total_b = gram_b[0:16, :]
    for j in range(1, n_ja):
        total_b = total_b + gram_b[16 * j : 16 * j + 16, :]
    at_half = pl.ds(pl.multiple_of(core * 16, 16), 16)
    matrix[at_half, :] = total_b * total_c
    send(matrix.at[at_half], matrix.at[at_half], 6, along_x(0, 1))
    part = matrix.at[pl.ds(0, 16)]
    sent.append((part, 6))
    wait(part, recv_sem.at[6])
    packed = matrix[...]
    square = jnp.concatenate([packed, pltpu.roll(packed, 64, 1)], axis=0)
    row64 = lax.broadcasted_iota(jnp.int32, (64, 128), 0)
    lane64 = lane[:64]
    state = jnp.where(lane64 < 64, square, jnp.where(lane64 - 64 == row64, 1.0, 0.0))
    state, recips = eliminate(state)
    inverse = jnp.where(lane64 < 64, pltpu.roll(state, 64, 1), state)

    wait(part_r, recv_sem.at[5])
    right = jnp.sum(partials[:, 0, :], axis=0, keepdims=True)
    products = inverse * right
    first = jnp.sum(jnp.where(lane64 < 64, products, 0.0), axis=1, keepdims=True)
    second = jnp.sum(jnp.where(lane64 < 64, 0.0, products), axis=1, keepdims=True)
    middle = jnp.where(lane64 < 64, first, second) * recips
    answer = jnp.sum(inverse * middle, axis=0, keepdims=True)
    out_ref[0, 0:1, :] = answer[:, :64]
    out_ref[0, 1:2, :] = answer[:, 64:]

    for part, stage in sent:
        wait(part, send_sem.at[stage])


def shards(sizes, tensor, factor_b, factor_c):
    n_ia, n_ja, n_ka = sizes
    arrays = (tensor, jnp.transpose(factor_b, (1, 2, 0)), jnp.transpose(factor_c, (1, 2, 0)))
    in_hbm = pl.BlockSpec(memory_space=pltpu.HBM)
    out = pl.pallas_call(
        functools.partial(kernel, sizes),
        name="als_update",
        out_shape=jax.ShapeDtypeStruct((1, 2, 64), F32),
        in_specs=[in_hbm, in_hbm, in_hbm],
        out_specs=pl.BlockSpec(memory_space=pltpu.VMEM),
        scratch_shapes=[
            pltpu.VMEM((128, 128, 128), BF16),
            pltpu.VMEM((1, 1, 64), BF16),
            pltpu.VMEM((1, 4, 64), BF16),
            pltpu.VMEM((8, 128), F32),
            pltpu.VMEM((8 * n_ia, 128), F32),
            pltpu.VMEM((8, 128), F32),
            pltpu.VMEM((32, 128), BF16),
            pltpu.VMEM((8 * n_ka, 128), F32),
            pltpu.VMEM((2 * 32 * n_ja, 128), BF16),
            pltpu.VMEM((32 * n_ja, 128), F32),
            pltpu.VMEM((16 * n_ja, 128), F32),
            pltpu.VMEM((16 * n_ka // 2, 128), F32),
            pltpu.VMEM((32, 128), F32),
            pltpu.VMEM((n_ja * n_ka, 128, 128), F32),
            pltpu.VMEM((n_ja * n_ka, 8, 128), F32),
            pltpu.VMEM((n_ja * n_ka, 8, 128), F32),
            pltpu.SemaphoreType.DMA((3,)),
            pltpu.SemaphoreType.REGULAR((2,)),
            pltpu.SemaphoreType.DMA((7,)),
            pltpu.SemaphoreType.DMA((7,)),
        ],
        compiler_params=pltpu.CompilerParams(
            collective_id=0, has_side_effects=True, vmem_limit_bytes=48 * 1024 * 1024
        ),
    )(*(pltpu.with_memory_space_constraint(array, pltpu.HBM) for array in arrays))
    return jnp.transpose(out, (2, 0, 1))


def solution(mesh):
    sizes = tuple(mesh.shape[a] for a in ("ia", "ja", "ka"))
    in_specs = (P("ia", "ja", "ka"), P(None, "ja", ("ia", "ka")), P(None, "ka", ("ia", "ja")))
    out_specs = P(None, "ia", ("ja", "ka"))
    return jax.shard_map(
        functools.partial(shards, sizes), mesh=mesh, in_specs=in_specs, out_specs=out_specs, check_vma=False
    )
```

```python
import functools

import jax
import jax.numpy as jnp
from jax import lax
from jax.experimental import pallas as pl
from jax.experimental.pallas import tpu as pltpu
from jax.sharding import PartitionSpec as P

MESH = pl.DeviceIdType.MESH
F32 = jnp.float32
BF16 = jnp.bfloat16
BLOCK = 16


def eliminate(state):
    rank = state.shape[0]
    row_of = lax.broadcasted_iota(jnp.int32, (rank, 128), 0)
    recips = jnp.zeros((rank, 128), F32)
    for first in range(0, rank, BLOCK):
        base = first // 8 * 8
        live = state[base:]
        rows = row_of[base:]
        columns = [jnp.broadcast_to(live[:, first + q : first + q + 1], live.shape) for q in range(BLOCK)]
        marks = recips[base:]
        for q in range(BLOCK):
            at = first + q - base
            recip = 1.0 / columns[q][at : at + 1]
            marks = jnp.where(rows == first + q, recip, marks)
            lower = jnp.where(rows > first + q, columns[q] * recip, 0.0)
            for later in range(q + 1, BLOCK):
                columns[later] = columns[later] - lower * columns[later][at : at + 1]
            live = live - lower * live[at : at + 1]
        state = live if base == 0 else jnp.concatenate([state[:base], live], axis=0)
        recips = marks if base == 0 else jnp.concatenate([recips[:base], marks], axis=0)
    return state, recips


def far_first(count):
    return sorted(range(1, count), key=lambda d: -min(d, count - d))


def kernel(
    sizes, tensor_ref, b_ref, c_ref, out_ref,
    tensor, own_b, own_c, piece, seen, tile_b, tile_c, slab_b, slab_c, wide_c, gram_b, gram_c, matrix, inner, partial, partials,
    load_sem, ready, send_sem, recv_sem,
):
    n_ia, n_ja, n_ka = sizes
    n_z = n_ka // 2
    ia, ja, ka = (lax.axis_index(a) for a in ("ia", "ja", "ka"))
    z, core = lax.div(ka, 2), lax.rem(ka, 2)
    n_own = n_ja * n_ka
    half = n_z // 2

    load_c = pltpu.make_async_copy(c_ref, own_c, load_sem.at[0])
    load_b = pltpu.make_async_copy(b_ref, own_b, load_sem.at[1])
    load = pltpu.make_async_copy(tensor_ref, tensor, load_sem.at[2])
    load_c.start()
    load_b.start()

    def along_y(d):
        return {"ia": lax.rem(ia + d, n_ia)}

    def along_x(dx, dc):
        return {"ja": lax.rem(ja + dx, n_ja), "ka": 2 * z + lax.rem(core + dc, 2)}

    ys = far_first(n_ia)
    xs = [(dx, dc) for dx in far_first(n_ja) + [0] for dc in (0, 1) if dx or dc]

    barrier = pltpu.get_barrier_semaphore()

    def signal(sem, place):
        pl.semaphore_signal(sem, inc=1, device_id=place, device_id_type=MESH)

    for d in ys:
        signal(barrier, along_y(d))
    signal(barrier, along_x(0, 1))

    def greet_higher_x(x, _):
        for c in (0, 1):
            signal(barrier, {"ja": x, "ka": 2 * z + c})
        return 0

    lax.fori_loop(ja + 1, n_ja, greet_higher_x, 0)

    def greet_higher(k, _):
        signal(barrier, {"ka": k})
        return 0

    lax.fori_loop(2 * z + 2, n_ka, greet_higher, 0)
    load.start()

    load_c.wait()
    load_b.wait()
    lane = lax.broadcasted_iota(jnp.int32, (128, 128), 1)
    c_rows = own_c[0].astype(F32)
    b_row = own_b[0].astype(F32)
    piece[0:4, :] = jnp.concatenate([c_rows, c_rows], axis=1)
    piece[4:5, :] = jnp.concatenate([b_row, b_row], axis=1)
    seen[pl.ds(pl.multiple_of(ia * 8, 8), 8), :] = piece[...]

    pl.semaphore_wait(barrier, n_ia + 2 * ja + 2 * z)

    def greet_lower(k, _):
        signal(ready.at[0], {"ka": k})
        return 0

    def greet_lower_x(x, _):
        for c in (0, 1):
            signal(ready.at[1], {"ja": x, "ka": 2 * z + c})
        return 0

    sent = []

    def send(source, target, stage, place):
        pltpu.make_async_remote_copy(
            src_ref=source, dst_ref=target, send_sem=send_sem.at[stage], recv_sem=recv_sem.at[stage],
            device_id=place, device_id_type=MESH,
        ).start()

    def wait(part, sem):
        pltpu.make_async_copy(part, part, sem).wait()

    for d in ys:
        send(piece, seen.at[pl.ds(pl.multiple_of(ia * 8, 8), 8)], 0, along_y(d))
    lax.fori_loop(0, 2 * z, greet_lower, 0)
    lax.fori_loop(0, ja, greet_lower_x, 0)
    part = seen.at[pl.ds(0, 8 * (n_ia - 1))]
    sent.append((part, 0))
    wait(part, recv_sem.at[0])

    @pl.when(ja < n_ja - 1)
    def _():
        pl.semaphore_wait(ready.at[1], 2 * (n_ja - 1 - ja))


    at_b = pl.ds(pl.multiple_of(ka * 8, 8), 8)
    at_c = pl.ds(pl.multiple_of((core * n_ja + ja) * 32, 32), 32)
    tile_c[...] = jnp.concatenate([seen[pl.ds(q, 8, stride=8), :] for q in range(4)], axis=0).astype(BF16)
    tile_b[...] = seen[pl.ds(4, 8, stride=8), :]
    for dx, dc in xs:
        send(tile_c, slab_c.at[at_c], 1, along_x(dx, dc))

    def send_b(k, _):
        send(tile_b, slab_b.at[at_b], 2, {"ka": k})
        return 0

    lax.fori_loop(0, 2 * z, send_b, 0)
    send_b(2 * z + 1 - core, 0)

    @pl.when(z < n_z - 1)
    def _():
        pl.semaphore_wait(ready.at[0], n_ka - 2 - 2 * z)

    lax.fori_loop(2 * z + 2, n_ka, send_b, 0)
    slab_c[at_c, :] = tile_c[...]
    slab_b[at_b, :] = tile_b[...]
    part = slab_c.at[pl.ds(0, 32 * (2 * n_ja - 1))]
    sent.append((part, 1))
    wait(part, recv_sem.at[1])

    def packed_gram(rows):
        full = lax.dot_general(rows, rows, (((0,), (0,)), ((), ())), preferred_element_type=F32)
        both = jnp.where(lane[:32] < 64, full[0:32], full[32:64])
        return jnp.where(core == 0, both[0:16], both[16:32])

    at_gram_c = pl.ds(pl.multiple_of(z * 16, 16), 16)
    at_gram_b = pl.ds(pl.multiple_of(ja * 16, 16), 16)
    gram_c[at_gram_c, :] = packed_gram(slab_c[...])
    wide_c[...] = slab_c[pl.ds(pl.multiple_of(core * n_ja * 32, 32), n_ja * 32), :].astype(F32)
    order_c = jnp.concatenate([wide_c[pl.ds(i, 16, stride=8), :] for i in range(8)], axis=0)
    weights = jnp.concatenate(
        [jnp.where(lane < 64, order_c, 0.0), jnp.where(lane >= 64, order_c, 0.0)], axis=0
    ).astype(BF16)

    def send_gram(to_z, _):
        @pl.when(to_z != z)
        def _():
            send(gram_c.at[at_gram_c], gram_c.at[at_gram_c], 3, {"ka": 2 * to_z + core})

        return 0

    lax.fori_loop(0, n_z, send_gram, 0)
    part_c = gram_c.at[pl.ds(0, 16 * (n_z - 1))]
    load.wait()

    def product(p):
        both = jnp.concatenate([tensor[2 * p], tensor[2 * p + 1]], axis=1)
        return jnp.dot(both, weights, preferred_element_type=F32)

    def contract(p, _):
        inner[p] = product(p)
        return 0

    @pl.when(z < half)
    def _():
        lax.fori_loop(0, n_own, contract, 0, unroll=4)

    part = slab_b.at[pl.ds(0, 8 * (n_ka - 1))]
    sent.append((part, 2))
    wait(part, recv_sem.at[2])

    def share_gram_b():
        gram_b[at_gram_b, :] = packed_gram(slab_b[...].astype(BF16))
        for d in far_first(n_ja):
            send(gram_b.at[at_gram_b], gram_b.at[at_gram_b], 4, along_x(d, 0))

    part_b = gram_b.at[pl.ds(0, 16 * (n_ja - 1))]

    order_b = jnp.concatenate([slab_b[pl.ds(i, 16, stride=8), :] for i in range(8)], axis=0)
    me = ja * n_ka + ka

    def weigh(made, to_z, _):
        owners = [
            (dx, dc, lax.rem(ja + dx, n_ja), 2 * to_z + lax.rem(core + dc, 2))
            for dx in far_first(n_ja) + [0]
            for dc in (1, 0)
        ]
        for dx, dc, x, k in owners:
            p = x * n_ka + k
            partial[p, 0:1, :] = jnp.sum(made(p) * order_b, axis=0, keepdims=True)
        for dx, dc, x, k in owners:
            p = x * n_ka + k

            def hand(x=x, k=k, p=p):
                send(partial.at[p, pl.ds(0, 1)], partials.at[pl.ds(me, 1)], 5, {"ja": x, "ka": k})

            if dx or dc:
                hand()
            else:
                pl.when(to_z != z)(hand)
        return 0

    @pl.when(z < half)
    def _():
        share_gram_b()
        lax.fori_loop(0, n_z, functools.partial(weigh, lambda p: inner[p]), 0)

    @pl.when(z >= half)
    def _():
        lax.fori_loop(0, n_z, functools.partial(weigh, product), 0)
        share_gram_b()

    partials[pl.ds(me, 1), :] = partial[me, 0:1, :]
    part_r = partials.at[pl.ds(0, n_own - 1)]
    sent += [(part_c, 3), (part_b, 4), (part_r, 5)]

    wait(part_c, recv_sem.at[3])
    total_c = gram_c[0:16, :]
    for k in range(1, n_z):
        total_c = total_c + gram_c[16 * k : 16 * k + 16, :]
    wait(part_b, recv_sem.at[4])
    total_b = gram_b[0:16, :]
    for j in range(1, n_ja):
        total_b = total_b + gram_b[16 * j : 16 * j + 16, :]
    at_half = pl.ds(pl.multiple_of(core * 16, 16), 16)
    matrix[at_half, :] = total_b * total_c
    send(matrix.at[at_half], matrix.at[at_half], 6, along_x(0, 1))
    part = matrix.at[pl.ds(0, 16)]
    sent.append((part, 6))
    wait(part, recv_sem.at[6])
    packed = matrix[...]
    square = jnp.concatenate([packed, pltpu.roll(packed, 64, 1)], axis=0)
    row64 = lax.broadcasted_iota(jnp.int32, (64, 128), 0)
    lane64 = lane[:64]
    state = jnp.where(lane64 < 64, square, jnp.where(lane64 - 64 == row64, 1.0, 0.0))
    state, recips = eliminate(state)
    inverse = jnp.where(lane64 < 64, pltpu.roll(state, 64, 1), state)

    wait(part_r, recv_sem.at[5])
    right = jnp.sum(partials[...], axis=0, keepdims=True)
    products = inverse * right
    first = jnp.sum(jnp.where(lane64 < 64, products, 0.0), axis=1, keepdims=True)
    second = jnp.sum(jnp.where(lane64 < 64, 0.0, products), axis=1, keepdims=True)
    middle = jnp.where(lane64 < 64, first, second) * recips
    answer = jnp.sum(inverse * middle, axis=0, keepdims=True)
    out_ref[0, 0:1, :] = answer[:, :64]
    out_ref[0, 1:2, :] = answer[:, 64:]

    for part, stage in sent:
        wait(part, send_sem.at[stage])


def shards(sizes, tensor, factor_b, factor_c):
    n_ia, n_ja, n_ka = sizes
    arrays = (tensor, jnp.transpose(factor_b, (1, 2, 0)), jnp.transpose(factor_c, (1, 2, 0)))
    in_hbm = pl.BlockSpec(memory_space=pltpu.HBM)
    out = pl.pallas_call(
        functools.partial(kernel, sizes),
        name="als_update",
        out_shape=jax.ShapeDtypeStruct((1, 2, 64), F32),
        in_specs=[in_hbm, in_hbm, in_hbm],
        out_specs=pl.BlockSpec(memory_space=pltpu.VMEM),
        scratch_shapes=[
            pltpu.VMEM((128, 128, 128), BF16),
            pltpu.VMEM((1, 1, 64), BF16),
            pltpu.VMEM((1, 4, 64), BF16),
            pltpu.VMEM((8, 128), F32),
            pltpu.VMEM((8 * n_ia, 128), F32),
            pltpu.VMEM((8, 128), F32),
            pltpu.VMEM((32, 128), BF16),
            pltpu.VMEM((8 * n_ka, 128), F32),
            pltpu.VMEM((2 * 32 * n_ja, 128), BF16),
            pltpu.VMEM((32 * n_ja, 128), F32),
            pltpu.VMEM((16 * n_ja, 128), F32),
            pltpu.VMEM((16 * n_ka // 2, 128), F32),
            pltpu.VMEM((32, 128), F32),
            pltpu.VMEM((n_ja * n_ka, 128, 128), F32),
            pltpu.VMEM((n_ja * n_ka, 8, 128), F32),
            pltpu.VMEM((n_ja * n_ka, 128), F32),
            pltpu.SemaphoreType.DMA((3,)),
            pltpu.SemaphoreType.REGULAR((2,)),
            pltpu.SemaphoreType.DMA((7,)),
            pltpu.SemaphoreType.DMA((7,)),
        ],
        compiler_params=pltpu.CompilerParams(
            collective_id=0, has_side_effects=True, vmem_limit_bytes=48 * 1024 * 1024
        ),
    )(*(pltpu.with_memory_space_constraint(array, pltpu.HBM) for array in arrays))
    return jnp.transpose(out, (2, 0, 1))


def solution(mesh):
    sizes = tuple(mesh.shape[a] for a in ("ia", "ja", "ka"))
    in_specs = (P("ia", "ja", "ka"), P(None, "ja", ("ia", "ka")), P(None, "ka", ("ia", "ja")))
    out_specs = P(None, "ia", ("ja", "ka"))
    return jax.shard_map(
        functools.partial(shards, sizes), mesh=mesh, in_specs=in_specs, out_specs=out_specs, check_vma=False
    )
```

```python
import functools

import jax
import jax.numpy as jnp
from jax import lax
from jax.experimental import pallas as pl
from jax.experimental.pallas import tpu as pltpu
from jax.sharding import PartitionSpec as P

MESH = pl.DeviceIdType.MESH
F32 = jnp.float32
BF16 = jnp.bfloat16
BLOCK = 16


def eliminate(state):
    rank = state.shape[0]
    row_of = lax.broadcasted_iota(jnp.int32, (rank, 128), 0)
    recips = jnp.zeros((rank, 128), F32)
    for first in range(0, rank, BLOCK):
        base = first // 8 * 8
        live = state[base:]
        rows = row_of[base:]
        columns = [jnp.broadcast_to(live[:, first + q : first + q + 1], live.shape) for q in range(BLOCK)]
        marks = recips[base:]
        for q in range(BLOCK):
            at = first + q - base
            recip = 1.0 / columns[q][at : at + 1]
            marks = jnp.where(rows == first + q, recip, marks)
            lower = jnp.where(rows > first + q, columns[q] * recip, 0.0)
            for later in range(q + 1, BLOCK):
                columns[later] = columns[later] - lower * columns[later][at : at + 1]
            live = live - lower * live[at : at + 1]
        state = live if base == 0 else jnp.concatenate([state[:base], live], axis=0)
        recips = marks if base == 0 else jnp.concatenate([recips[:base], marks], axis=0)
    return state, recips


def far_first(count):
    return sorted(range(1, count), key=lambda d: -min(d, count - d))


def kernel(
    sizes, tensor_ref, b_ref, c_ref, out_ref,
    tensor, own_b, own_c, piece, seen, tile_b, tile_c, slab_b, slab_c, wide_c, gram_b, gram_c, matrix, inner, partial, partials,
    load_sem, ready, send_sem, recv_sem,
):
    n_ia, n_ja, n_ka = sizes
    n_z = n_ka // 2
    ia, ja, ka = (lax.axis_index(a) for a in ("ia", "ja", "ka"))
    z, core = lax.div(ka, 2), lax.rem(ka, 2)
    n_own = n_ja * n_ka
    half = n_z // 2

    load_c = pltpu.make_async_copy(c_ref, own_c, load_sem.at[0])
    load_b = pltpu.make_async_copy(b_ref, own_b, load_sem.at[1])
    load = pltpu.make_async_copy(tensor_ref, tensor, load_sem.at[2])
    load_c.start()
    load_b.start()

    def along_y(d):
        return {"ia": lax.rem(ia + d, n_ia)}

    def along_x(dx, dc):
        return {"ja": lax.rem(ja + dx, n_ja), "ka": 2 * z + lax.rem(core + dc, 2)}

    ys = far_first(n_ia)
    xs = [(dx, dc) for dx in far_first(n_ja) + [0] for dc in (0, 1) if dx or dc]

    barrier = pltpu.get_barrier_semaphore()

    def signal(sem, place):
        pl.semaphore_signal(sem, inc=1, device_id=place, device_id_type=MESH)

    for d in ys:
        signal(barrier, along_y(d))
    signal(barrier, along_x(0, 1))

    def greet_higher_x(x, _):
        for c in (0, 1):
            signal(barrier, {"ja": x, "ka": 2 * z + c})
        return 0

    lax.fori_loop(ja + 1, n_ja, greet_higher_x, 0)

    def greet_higher(k, _):
        signal(barrier, {"ka": k})
        return 0

    lax.fori_loop(2 * z + 2, n_ka, greet_higher, 0)

    def greet_half(k, _):
        for d in ys:
            signal(barrier, {"ia": lax.rem(ia + d, n_ia), "ka": k})
        return 0

    @pl.when(z < half)
    def _():
        lax.fori_loop(2 * half, n_ka, greet_half, 0)

    load.start()

    load_c.wait()
    load_b.wait()
    lane = lax.broadcasted_iota(jnp.int32, (128, 128), 1)
    c_rows = own_c[0].astype(F32)
    b_row = own_b[0].astype(F32)
    piece[0:4, :] = jnp.concatenate([c_rows, c_rows], axis=1)
    piece[4:5, :] = jnp.concatenate([b_row, b_row], axis=1)
    seen[pl.ds(pl.multiple_of(ia * 8, 8), 8), :] = piece[...]

    far = jnp.where(z < half, 0, 2 * half * (n_ia - 1))
    pl.semaphore_wait(barrier, n_ia + 2 * ja + 2 * z + far)

    def greet_lower(k, _):
        signal(ready.at[0], {"ka": k})
        return 0

    def greet_lower_x(x, _):
        for c in (0, 1):
            signal(ready.at[1], {"ja": x, "ka": 2 * z + c})
        return 0

    sent = []

    def send(source, target, stage, place):
        pltpu.make_async_remote_copy(
            src_ref=source, dst_ref=target, send_sem=send_sem.at[stage], recv_sem=recv_sem.at[stage],
            device_id=place, device_id_type=MESH,
        ).start()

    def wait(part, sem):
        pltpu.make_async_copy(part, part, sem).wait()

    for d in ys:
        send(piece, seen.at[pl.ds(pl.multiple_of(ia * 8, 8), 8)], 0, along_y(d))
    lax.fori_loop(0, 2 * z, greet_lower, 0)
    lax.fori_loop(0, ja, greet_lower_x, 0)

    at_own = pl.ds(ka * 8 + ia, 1)

    def send_row(k, _):
        for d in ys + [0]:
            send(piece.at[pl.ds(4, 1)], slab_b.at[at_own], 2, {"ia": lax.rem(ia + d, n_ia), "ka": k})
        return 0

    @pl.when(z >= half)
    def _():
        lax.fori_loop(0, 2 * half, send_row, 0)

    part = seen.at[pl.ds(0, 8 * (n_ia - 1))]
    sent.append((part, 0))
    wait(part, recv_sem.at[0])

    @pl.when(ja < n_ja - 1)
    def _():
        pl.semaphore_wait(ready.at[1], 2 * (n_ja - 1 - ja))

    def vouch(k, _):
        signal(ready.at[2], {"ka": k})
        return 0

    @pl.when(z >= half)
    def _():
        lax.fori_loop(0, 2 * half, vouch, 0)


    at_b = pl.ds(pl.multiple_of(ka * 8, 8), 8)
    at_c = pl.ds(pl.multiple_of((core * n_ja + ja) * 32, 32), 32)
    tile_c[...] = jnp.concatenate([seen[pl.ds(q, 8, stride=8), :] for q in range(4)], axis=0).astype(BF16)
    tile_b[...] = seen[pl.ds(4, 8, stride=8), :]
    for dx, dc in xs:
        send(tile_c, slab_c.at[at_c], 1, along_x(dx, dc))

    def send_b(k, _):
        send(tile_b, slab_b.at[at_b], 2, {"ka": k})
        return 0

    lax.fori_loop(jnp.where(z < half, 0, 2 * half), 2 * z, send_b, 0)
    send_b(2 * z + 1 - core, 0)

    @pl.when(z < n_z - 1)
    def _():
        pl.semaphore_wait(ready.at[0], n_ka - 2 - 2 * z)

    lax.fori_loop(2 * z + 2, n_ka, send_b, 0)
    slab_c[at_c, :] = tile_c[...]
    slab_b[at_b, :] = tile_b[...]
    part = slab_c.at[pl.ds(0, 32 * (2 * n_ja - 1))]
    sent.append((part, 1))
    wait(part, recv_sem.at[1])

    def packed_gram(rows):
        full = lax.dot_general(rows, rows, (((0,), (0,)), ((), ())), preferred_element_type=F32)
        both = jnp.where(lane[:32] < 64, full[0:32], full[32:64])
        return jnp.where(core == 0, both[0:16], both[16:32])

    at_gram_c = pl.ds(pl.multiple_of(z * 16, 16), 16)
    at_gram_b = pl.ds(pl.multiple_of(ja * 16, 16), 16)
    gram_c[at_gram_c, :] = packed_gram(slab_c[...])
    wide_c[...] = slab_c[pl.ds(pl.multiple_of(core * n_ja * 32, 32), n_ja * 32), :].astype(F32)
    order_c = jnp.concatenate([wide_c[pl.ds(i, 16, stride=8), :] for i in range(8)], axis=0)
    weights = jnp.concatenate(
        [jnp.where(lane < 64, order_c, 0.0), jnp.where(lane >= 64, order_c, 0.0)], axis=0
    ).astype(BF16)

    def send_gram(to_z, _):
        @pl.when(to_z != z)
        def _():
            send(gram_c.at[at_gram_c], gram_c.at[at_gram_c], 3, {"ka": 2 * to_z + core})

        return 0

    lax.fori_loop(0, n_z, send_gram, 0)
    part_c = gram_c.at[pl.ds(0, 16 * (n_z - 1))]
    load.wait()

    def product(p):
        both = jnp.concatenate([tensor[2 * p], tensor[2 * p + 1]], axis=1)
        return jnp.dot(both, weights, preferred_element_type=F32)

    def contract(p, _):
        inner[p] = product(p)
        return 0

    @pl.when(z < half)
    def _():
        lax.fori_loop(0, n_own, contract, 0, unroll=4)

    part = slab_b.at[pl.ds(0, 8 * (n_ka - 1))]
    sent.append((part, 2))
    wait(part, recv_sem.at[2])

    def share_gram_b():
        gram_b[at_gram_b, :] = packed_gram(slab_b[...].astype(BF16))
        for d in far_first(n_ja):
            send(gram_b.at[at_gram_b], gram_b.at[at_gram_b], 4, along_x(d, 0))

    part_b = gram_b.at[pl.ds(0, 16 * (n_ja - 1))]

    @pl.when(z < half)
    def _():
        pl.semaphore_wait(ready.at[2], n_ka - 2 * half)

    order_b = jnp.concatenate([slab_b[pl.ds(i, 16, stride=8), :] for i in range(8)], axis=0)
    me = ja * n_ka + ka

    def weigh(made, to_z, _):
        owners = [
            (dx, dc, lax.rem(ja + dx, n_ja), 2 * to_z + lax.rem(core + dc, 2))
            for dx in far_first(n_ja) + [0]
            for dc in (1, 0)
        ]
        for dx, dc, x, k in owners:
            p = x * n_ka + k
            partial[p, 0:1, :] = jnp.sum(made(p) * order_b, axis=0, keepdims=True)
        for dx, dc, x, k in owners:
            p = x * n_ka + k

            def hand(x=x, k=k, p=p):
                send(partial.at[p, pl.ds(0, 1)], partials.at[pl.ds(me, 1)], 5, {"ja": x, "ka": k})

            if dx or dc:
                hand()
            else:
                pl.when(to_z != z)(hand)
        return 0

    @pl.when(z < half)
    def _():
        weigh(lambda p: inner[p], 0, 0)
        share_gram_b()
        lax.fori_loop(1, n_z, functools.partial(weigh, lambda p: inner[p]), 0)

    @pl.when(z >= half)
    def _():
        lax.fori_loop(0, n_z, functools.partial(weigh, product), 0)
        share_gram_b()

    partials[pl.ds(me, 1), :] = partial[me, 0:1, :]
    part_r = partials.at[pl.ds(0, n_own - 1)]
    sent += [(part_c, 3), (part_b, 4), (part_r, 5)]

    wait(part_c, recv_sem.at[3])
    total_c = gram_c[0:16, :]
    for k in range(1, n_z):
        total_c = total_c + gram_c[16 * k : 16 * k + 16, :]
    wait(part_b, recv_sem.at[4])
    total_b = gram_b[0:16, :]
    for j in range(1, n_ja):
        total_b = total_b + gram_b[16 * j : 16 * j + 16, :]
    at_half = pl.ds(pl.multiple_of(core * 16, 16), 16)
    matrix[at_half, :] = total_b * total_c
    send(matrix.at[at_half], matrix.at[at_half], 6, along_x(0, 1))
    part = matrix.at[pl.ds(0, 16)]
    sent.append((part, 6))
    wait(part, recv_sem.at[6])
    packed = matrix[...]
    square = jnp.concatenate([packed, pltpu.roll(packed, 64, 1)], axis=0)
    row64 = lax.broadcasted_iota(jnp.int32, (64, 128), 0)
    lane64 = lane[:64]
    state = jnp.where(lane64 < 64, square, jnp.where(lane64 - 64 == row64, 1.0, 0.0))
    state, recips = eliminate(state)
    inverse = jnp.where(lane64 < 64, pltpu.roll(state, 64, 1), state)

    wait(part_r, recv_sem.at[5])
    right = jnp.sum(partials[...], axis=0, keepdims=True)
    products = inverse * right
    first = jnp.sum(jnp.where(lane64 < 64, products, 0.0), axis=1, keepdims=True)
    second = jnp.sum(jnp.where(lane64 < 64, 0.0, products), axis=1, keepdims=True)
    middle = jnp.where(lane64 < 64, first, second) * recips
    answer = jnp.sum(inverse * middle, axis=0, keepdims=True)
    out_ref[0, 0:1, :] = answer[:, :64]
    out_ref[0, 1:2, :] = answer[:, 64:]

    for part, stage in sent:
        wait(part, send_sem.at[stage])


def shards(sizes, tensor, factor_b, factor_c):
    n_ia, n_ja, n_ka = sizes
    arrays = (tensor, jnp.transpose(factor_b, (1, 2, 0)), jnp.transpose(factor_c, (1, 2, 0)))
    in_hbm = pl.BlockSpec(memory_space=pltpu.HBM)
    out = pl.pallas_call(
        functools.partial(kernel, sizes),
        name="als_update",
        out_shape=jax.ShapeDtypeStruct((1, 2, 64), F32),
        in_specs=[in_hbm, in_hbm, in_hbm],
        out_specs=pl.BlockSpec(memory_space=pltpu.VMEM),
        scratch_shapes=[
            pltpu.VMEM((128, 128, 128), BF16),
            pltpu.VMEM((1, 1, 64), BF16),
            pltpu.VMEM((1, 4, 64), BF16),
            pltpu.VMEM((8, 128), F32),
            pltpu.VMEM((8 * n_ia, 128), F32),
            pltpu.VMEM((8, 128), F32),
            pltpu.VMEM((32, 128), BF16),
            pltpu.VMEM((8 * n_ka, 128), F32),
            pltpu.VMEM((2 * 32 * n_ja, 128), BF16),
            pltpu.VMEM((32 * n_ja, 128), F32),
            pltpu.VMEM((16 * n_ja, 128), F32),
            pltpu.VMEM((16 * n_ka // 2, 128), F32),
            pltpu.VMEM((32, 128), F32),
            pltpu.VMEM((n_ja * n_ka, 128, 128), F32),
            pltpu.VMEM((n_ja * n_ka, 8, 128), F32),
            pltpu.VMEM((n_ja * n_ka, 128), F32),
            pltpu.SemaphoreType.DMA((3,)),
            pltpu.SemaphoreType.REGULAR((3,)),
            pltpu.SemaphoreType.DMA((7,)),
            pltpu.SemaphoreType.DMA((7,)),
        ],
        compiler_params=pltpu.CompilerParams(
            collective_id=0, has_side_effects=True, vmem_limit_bytes=48 * 1024 * 1024
        ),
    )(*(pltpu.with_memory_space_constraint(array, pltpu.HBM) for array in arrays))
    return jnp.transpose(out, (2, 0, 1))


def solution(mesh):
    sizes = tuple(mesh.shape[a] for a in ("ia", "ja", "ka"))
    in_specs = (P("ia", "ja", "ka"), P(None, "ja", ("ia", "ka")), P(None, "ka", ("ia", "ja")))
    out_specs = P(None, "ia", ("ja", "ka"))
    return jax.shard_map(
        functools.partial(shards, sizes), mesh=mesh, in_specs=in_specs, out_specs=out_specs, check_vma=False
    )
```
